32 devices in a mesh: ctx: 8 (over y, x, core), head: 4 (over z).
Axes of the slice: x: 2, y: 2, z: 4, core: 2. Of those that a mesh axis runs over, the one named last changes fastest.
Arguments:
- queries: bfloat16 [8192, 512], P('ctx', 'head'), may hold values from -6 to 6
- keys: bfloat16 [8192, 512], P('ctx', 'head'), may hold values from -6 to 6
- values: bfloat16 [8192, 4096], P('ctx', 'head'), may hold values from -6 to 6
- conv_weight: float32 [3, 4096], P(None, 'head'), may hold values from -3 to 3
- gain: float32 [4096], P('head'), may hold values from 0.5 to 1.5
- cotangent: bfloat16 [8192, 4096], P('ctx', 'head'), may hold values from -6 to 6
Outputs:
- normed: bfloat16 [8192, 4096], P('ctx', 'head')
- grad_q: bfloat16 [8192, 512], P('ctx', 'head')
- grad_k: bfloat16 [8192, 512], P('ctx', 'head')
- grad_v: bfloat16 [8192, 4096], P('ctx', 'head')
The draws below stay inside these ranges and needn't reach their ends.
All inputs are finite; a program needn't handle non-finite values.
Results may differ from the reference program's by a relative error of at most 0.0068.
Values may be sent and summed in bfloat16 or wider, within the bound.
A program may use at most 192 MiB of HBM per device.

```python
import math
import jax
import jax.numpy as jnp
from jax import lax

HEADS = 32
FEAT = 16
DV = 128
CONV = 3
TOK_DEV = 1024
FEATS = 273
DMODEL = 4096
SEQ = 8192


def levels(own_key, extent, cuts, smallest, high):
    loudness, own = 1.0, jax.random.fold_in(own_key, 6)
    for dim, shards_of in cuts:
        heights = jnp.exp(jax.random.uniform(jax.random.fold_in(own, dim), (shards_of,), jnp.float32, smallest / len(cuts), high / len(cuts)))
        loudness = loudness * jnp.repeat(heights, extent[dim] // shards_of).reshape([-1 if axis == dim else 1 for axis in range(len(extent))])
    return loudness


def scatter_about(stream_key, dims, scale, limit, split=(), held_as=jnp.bfloat16):
    level = levels(stream_key, dims, split, -0.22, 0.18) if split else 1.0
    entries = jax.random.normal(stream_key, dims, jnp.float32) * scale * level
    return jnp.minimum(jnp.maximum(entries, -limit), limit).astype(held_as)


def setup_inputs(seed: int = 0) -> dict:
    key_list = jax.random.split(jax.random.key(seed), 7)
    queries = scatter_about(key_list[0], (SEQ, HEADS * FEAT), 1.0, 6.0, ((0, 8), (1, 4)))
    keys = scatter_about(key_list[1], (SEQ, HEADS * FEAT), 1.0, 6.0, ((0, 8), (1, 4)))
    values = scatter_about(key_list[2], (SEQ, DMODEL), 1.0, 6.0, ((0, 8), (1, 4)))
    conv_weight = scatter_about(key_list[3], (CONV, DMODEL), 0.6, 3.0, ((1, 4),), jnp.float32)
    gain = jnp.clip(1.0 + 0.1 * jax.random.normal(key_list[4], (DMODEL,), jnp.float32), 0.5, 1.5)
    cotangent = scatter_about(key_list[5], (SEQ, DMODEL), 1.0, 6.0, ((0, 8), (1, 4)))
    return dict(queries=queries, keys=keys, values=values, conv_weight=conv_weight, gain=gain, cotangent=cotangent)


scale_quad = 0.25 / math.sqrt(2.0)
eps_norm = 1e-06
highest = lax.Precision.HIGHEST

def rounded(array):
    return lax.optimization_barrier(array.astype(jnp.bfloat16)).astype(jnp.float32)

def feature_map(column):
    lead = column.shape[:-1]
    width = column.shape[-1]
    square = (column[..., :, None] * column[..., None, :]).reshape(lead + (width * width,)) * scale_quad
    return jnp.concatenate([jnp.ones(lead + (1,), jnp.float32), column * 0.5, square], axis=-1)

def feature_grad(grad_feat, column):
    width = column.shape[-1]
    lead = column.shape[:-1]
    linear_part = grad_feat[..., 1:1 + width] * 0.5
    square = grad_feat[..., 1 + width:].reshape(lead + (width, width))
    left = jnp.einsum('thij,thj->thi', square, column, precision=highest)
    right = jnp.einsum('thij,thi->thj', square, column, precision=highest)
    return linear_part + scale_quad * (left + right)

def block_kernel(query_f, key_f):
    dots = jnp.einsum('thf,shf->hts', query_f, key_f, precision=highest)
    length = dots.shape[1]
    causal = jnp.arange(length)[:, None] >= jnp.arange(length)[None, :]
    kernel = jnp.where(causal[None], 1.0 + dots * 0.25 + dots * dots / 32.0, jnp.zeros_like(dots))
    return (dots, causal, kernel)

def reference(queries, keys, values, conv_weight, gain, cotangent):
    seq_len = values.shape[0]
    blocks = seq_len // TOK_DEV
    value_f = values.astype(jnp.float32)
    conv_taps = conv_weight.astype(jnp.float32)
    mixed = jnp.zeros(value_f.shape, jnp.float32)
    for tap_index in range(CONV):
        shifted = jnp.concatenate([jnp.zeros((tap_index, value_f.shape[1]), jnp.float32), value_f[:seq_len - tap_index]], axis=0)
        mixed = mixed + conv_taps[tap_index] * shifted
    convolved = mixed.astype(jnp.bfloat16)
    query_blk = queries.reshape(blocks, TOK_DEV, HEADS, FEAT)
    key_blk = keys.reshape(blocks, TOK_DEV, HEADS, FEAT)
    conv_blk = convolved.reshape(blocks, TOK_DEV, HEADS, DV)

    def forward_step(carry, inputs):
        state, key_total = carry
        query_b, key_b, conv_b = inputs
        query_f = query_b.astype(jnp.float32)
        key_f = key_b.astype(jnp.float32)
        conv_f = conv_b.astype(jnp.float32)
        dots, causal, kernel = block_kernel(query_f, key_f)
        weights = rounded(kernel)
        query_feat = rounded(feature_map(query_f))
        key_feat = rounded(feature_map(key_f))
        state_r = rounded(state)
        numer = jnp.einsum('hts,shc->thc', weights, conv_f, precision=highest) + jnp.einsum('thm,hmc->thc', query_feat, state_r, precision=highest)
        denom = lax.optimization_barrier(jnp.sum(kernel, axis=2)).T + jnp.einsum('thm,hm->th', query_feat, key_total, precision=highest)
        new_state = state + jnp.einsum('thm,thc->hmc', key_feat, conv_f, precision=highest)
        new_total = key_total + lax.optimization_barrier(jnp.sum(key_feat, axis=0))
        return ((new_state, new_total), (numer, denom, state, key_total))
    start_state = (jnp.zeros((HEADS, FEATS, DV), jnp.float32), jnp.zeros((HEADS, FEATS), jnp.float32))
    last_unused, (numer, denom, states, key_totals) = lax.scan(forward_step, start_state, (query_blk, key_blk, conv_blk))
    attended = numer / denom[..., None]
    inv_rms = lax.rsqrt(lax.optimization_barrier(jnp.sum(attended * attended, axis=(2, 3))) / (HEADS * DV) + eps_norm)
    gain_cols = gain.reshape(HEADS, DV)
    normed = (attended * inv_rms[..., None, None] * gain_cols).astype(jnp.bfloat16).reshape(seq_len, HEADS * DV)
    upstream = cotangent.reshape(blocks, TOK_DEV, HEADS, DV).astype(jnp.float32) * gain_cols
    agree = lax.optimization_barrier(jnp.sum(upstream * attended, axis=(2, 3)))
    d_att = inv_rms[..., None, None] * upstream - attended * (inv_rms ** 3 * agree / (HEADS * DV))[..., None, None]
    numerator_grad = (d_att / denom[..., None]).astype(jnp.bfloat16)
    denominator_grad = -lax.optimization_barrier(jnp.sum(d_att * attended, axis=3)) / denom

    def backward_step(carry, inputs):
        later_state, later_total = carry
        query_b, key_b, conv_b, numer_g, denom_g, state, key_total = inputs
        query_f = query_b.astype(jnp.float32)
        key_f = key_b.astype(jnp.float32)
        conv_f = conv_b.astype(jnp.float32)
        numer_gf = numer_g.astype(jnp.float32)
        dots, causal, kernel = block_kernel(query_f, key_f)
        weights = rounded(kernel)
        query_feat = rounded(feature_map(query_f))
        key_feat = rounded(feature_map(key_f))
        pressure = jnp.einsum('thc,shc->hts', numer_gf, conv_f, precision=highest) + denom_g.T[:, :, None]
        d_kernel = rounded(jnp.where(causal[None], pressure * (0.25 + dots / 16.0), jnp.zeros_like(dots)))
        grad_q_in = jnp.einsum('hts,shf->thf', d_kernel, key_f, precision=highest)
        grad_k_in = jnp.einsum('hts,thf->shf', d_kernel, query_f, precision=highest)
        grad_c_in = jnp.einsum('hts,thc->shc', weights, numer_gf, precision=highest)
        state_r = rounded(state)
        later_r = rounded(later_state)
        query_fg = jnp.einsum('thc,hmc->thm', numer_gf, state_r, precision=highest) + denom_g[:, :, None] * key_total[None]
        key_fg = jnp.einsum('thc,hmc->thm', conv_f, later_r, precision=highest) + later_total[None]
        grad_q = (grad_q_in + feature_grad(query_fg, query_f)).astype(jnp.bfloat16)
        grad_k = (grad_k_in + feature_grad(key_fg, key_f)).astype(jnp.bfloat16)
        d_conv = (grad_c_in + jnp.einsum('thm,hmc->thc', key_feat, later_r, precision=highest)).astype(jnp.bfloat16)
        new_state = later_state + jnp.einsum('thm,thc->hmc', query_feat, numer_gf, precision=highest)
        new_total = later_total + jnp.einsum('thm,th->hm', query_feat, denom_g, precision=highest)
        return ((new_state, new_total), (grad_q, grad_k, d_conv))
    last_back, (grad_q, grad_k, d_conv) = lax.scan(backward_step, start_state, (query_blk, key_blk, conv_blk, numerator_grad, denominator_grad, states, key_totals), reverse=True)
    d_conv_f = d_conv.reshape(seq_len, HEADS * DV).astype(jnp.float32)
    grad_v = jnp.zeros(d_conv_f.shape, jnp.float32)
    for tap_index in range(CONV):
        shifted = jnp.concatenate([d_conv_f[tap_index:], jnp.zeros((tap_index, d_conv_f.shape[1]), jnp.float32)], axis=0)
        grad_v = grad_v + conv_taps[tap_index] * shifted
    return (normed, grad_q.reshape(seq_len, HEADS * FEAT), grad_k.reshape(seq_len, HEADS * FEAT), grad_v.astype(jnp.bfloat16))
```

```python
import functools
import math

import jax
import jax.numpy as jnp
from jax import lax
from jax.experimental import pallas as pl
from jax.experimental.pallas import tpu as pltpu
from jax.sharding import PartitionSpec as P

FEAT = 16
CONV = 3
ROWS = 160
TILE = 256
S = 0.25 / math.sqrt(2.0)
EPS = 1e-06
F32 = jnp.float32
BF = jnp.bfloat16
LIMIT = 56 * 1024 * 1024


def dot(a, b):
    return jnp.dot(a, b, preferred_element_type=F32)


def dot_nt(a, b):
    return lax.dot_general(a, b, (((1,), (1,)), ((), ())), preferred_element_type=F32)


def dot_tn(a, b):
    return lax.dot_general(a, b, (((0,), (0,)), ((), ())), preferred_element_type=F32)


def turned(x, d):
    return pltpu.roll(x, FEAT - d, 0)


def phi(x, pair):
    parts = [x * 0.5, (x * x) * S]
    for d in range(1, 8):
        parts.append((x * turned(x, d)) * (pair * S))
    parts.append((x[:8] * x[8:]) * (pair * S))
    row = lax.broadcasted_iota(jnp.int32, (8, x.shape[1]), 0)
    parts.append(jnp.where(row == 0, 1.0, 0.0).astype(F32))
    return jnp.concatenate(parts, axis=0).astype(BF)


def phi_grad(g, x):
    total = g[16:32] * x
    for d in range(1, 8):
        part = g[16 + 16 * d : 32 + 16 * d]
        total = total + part * turned(x, d) + pltpu.roll(part * x, d, 0)
    last = g[144:152]
    total = total + jnp.concatenate([last * x[8:], last * x[:8]], axis=0)
    return g[:16] * 0.5 + (2.0 * S) * total


def lanes(rows):
    return lax.broadcasted_iota(jnp.int32, (rows, 128), 1)


def with_ones(conv):
    ones = jnp.where(lanes(conv.shape[0]) < 2, 1.0, 0.0).astype(BF)
    return jnp.concatenate([conv, ones], axis=1)


def with_split(wide, column, order):
    high = column.astype(BF).astype(F32)
    low = column - high
    lane = lanes(wide.shape[0])
    right = jnp.zeros(lane.shape, F32)
    for at, kind in enumerate(order):
        right = jnp.where(lane == at, high if kind == "h" else low, right)
    return jnp.concatenate([wide.astype(BF), right.astype(BF)], axis=1)


def state_kernel(values_ref, prev_ref, taps_ref, kt_ref, conv_ref, state_ref):
    v = values_ref[...].astype(F32)
    row = lax.broadcasted_iota(jnp.int32, v.shape, 0)
    one = jnp.where(row == 0, prev_ref[1:2], pltpu.roll(v, 1, 0))
    two = jnp.where(
        row == 0, prev_ref[0:1], jnp.where(row == 1, prev_ref[1:2], pltpu.roll(v, 2, 0))
    )
    conv = (taps_ref[0:1] * v + taps_ref[1:2] * one + taps_ref[2:3] * two).astype(BF)
    conv_ref[...] = conv
    total = dot(phi(kt_ref[...].astype(F32), 1.0), with_ones(conv))
    state_ref[0] = with_split(total[:, :128], total[:, 128:129], "hl")


def head_rows(ref, h):
    row = lax.broadcasted_iota(jnp.int32, (ref.shape[0], 1), 0)
    return (ref[...].astype(F32) * jnp.where(row // FEAT == h, 1.0, 0.0)).astype(BF)


def head_lanes(ref, h):
    lane = lax.broadcasted_iota(jnp.int32, (1, ref.shape[1]), 1)
    return (ref[...].astype(F32) * jnp.where(lane // FEAT == h, 1.0, 0.0)).astype(BF)


def forward_kernel(
    index_ref, all_ref, q_ref, kt_ref, qth_ref, conv_ref, cot_ref, gain_ref,
    att_ref, den_ref, stat_ref, prior_ref, sums,
):
    h = pl.program_id(0)
    me = index_ref[0]
    total = jnp.zeros((ROWS, 256), F32)
    for j in range(all_ref.shape[0]):
        total = total + jnp.where(j < me, all_ref[j, 0].astype(F32), 0.0)
    prior = with_split(total[:, :128], total[:, 128:129] + total[:, 129:130], "hhl")
    prior_ref[0] = prior
    length = conv_ref.shape[0]
    kt = head_rows(kt_ref, h)
    conv = with_ones(conv_ref[...])
    inter = dot_tn(phi(qth_ref[...].astype(F32), 2.0), prior)
    causal = lax.broadcasted_iota(jnp.int32, (TILE, TILE), 0) >= lax.broadcasted_iota(
        jnp.int32, (TILE, TILE), 1
    )

    @pl.when(h == 0)
    def _():
        sums[...] = jnp.zeros_like(sums)
        den_ref[...] = jnp.zeros_like(den_ref)

    for t0 in range(0, length, TILE):
        q = q_ref[t0 : t0 + TILE]
        out = inter[t0 : t0 + TILE]
        d = dot(q, kt[:, t0 : t0 + TILE])
        w = jnp.where(causal, 1.0 + d * (0.25 + d * 0.03125), 0.0).astype(BF)
        out = out + dot(w, conv[t0 : t0 + TILE])
        if t0:
            d = dot(q, kt[:, :t0])
            w = (1.0 + d * (0.25 + d * 0.03125)).astype(BF)
            out = out + dot(w, conv[:t0])
        den = out[:, 128:129] + out[:, 130:131]
        att = out[:, :128] / den
        rows = slice(t0, t0 + TILE)
        att_ref[rows] = att
        lane = lanes(TILE)
        den_ref[rows] = jnp.where(lane == h, den, den_ref[rows])
        square = jnp.sum(att * att, axis=1, keepdims=True)
        agree = jnp.sum(
            att * (cot_ref[rows].astype(F32) * gain_ref[...]), axis=1, keepdims=True
        )
        sums[rows] += jnp.where(lane == 0, square, jnp.where(lane == 1, agree, 0.0))

    @pl.when(h == pl.num_programs(0) - 1)
    def _():
        stat_ref[...] = sums[...].T[:8]


def norm_kernel(
    width, att_ref, den_ref, stat_ref, cot_ref, gain_ref, qth_ref, normed_ref, dn_ref, back_ref
):
    h = pl.program_id(0)
    att = att_ref[...]
    gain = gain_ref[...]
    length = att.shape[0]
    den = jnp.sum(jnp.where(lanes(length) == h, den_ref[...], 0.0), axis=1, keepdims=True)
    inv = lax.rsqrt(stat_ref[:, 0:1] / width + EPS)
    shrink = inv * inv * inv * stat_ref[:, 1:2] / width
    normed_ref[...] = (att * inv * gain).astype(BF)
    d_att = inv * (cot_ref[...].astype(F32) * gain) - att * shrink
    each = 1.0 / den
    d_den = -jnp.sum(d_att * att, axis=1, keepdims=True) * each
    dn = with_split(d_att * each, d_den, "hlh")
    dn_ref[...] = dn
    total = dot(phi(qth_ref[...].astype(F32), 1.0), dn)
    back_ref[0] = with_split(total[:, :128], total[:, 128:129] + total[:, 129:130], "hl")


def backward_kernel(
    index_ref, all_ref, q_ref, k_ref, qt_ref, qth_ref, kth_ref, conv_ref, dn_ref, prior_ref,
    gq_ref, gk_ref, dconv_ref, acc_q, acc_kt, acc_k,
):
    h = pl.program_id(0)
    me = index_ref[0]
    total = jnp.zeros((ROWS, 256), F32)
    for j in range(all_ref.shape[0]):
        total = total + jnp.where(j > me, all_ref[j, 0].astype(F32), 0.0)
    later = with_split(total[:, :128], total[:, 128:129] + total[:, 129:130], "hl")
    length = conv_ref.shape[0]
    conv = with_ones(conv_ref[...])
    qt = head_rows(qt_ref, h)
    qm = head_lanes(q_ref, h)
    kth = kth_ref[...]
    kx = kth.astype(F32)
    qx = qth_ref[...].astype(F32)
    here = pl.ds(pl.multiple_of(h * FEAT, FEAT), FEAT)
    acc_q[here] = phi_grad(dot_nt(prior_ref[0], dn_ref[...]), qx)
    acc_kt[here] = phi_grad(dot_nt(later, conv), kx)
    inter = dot_tn(phi(kx, 2.0), later[:, :128])
    causal = lax.broadcasted_iota(jnp.int32, (TILE, TILE), 1) >= lax.broadcasted_iota(
        jnp.int32, (TILE, TILE), 0
    )

    @pl.when(h == 0)
    def _():
        acc_k[...] = jnp.zeros_like(acc_k)

    for s0 in range(0, length, TILE):
        rows = slice(s0, s0 + TILE)
        k = k_ref[rows]
        grad_c = inter[rows]
        grad_k = acc_k[rows]
        pieces = [slice(s0, s0 + TILE)]
        if s0 + TILE < length:
            pieces.append(slice(s0 + TILE, length))
        for at, cols in enumerate(pieces):
            d = dot(k, qt[:, cols])
            w = 1.0 + d * (0.25 + d * 0.03125)
            dk = dot_nt(conv[rows], dn_ref[cols]) * (0.25 + d * 0.0625)
            if at == 0:
                w = jnp.where(causal, w, 0.0)
                dk = jnp.where(causal, dk, 0.0)
            w = w.astype(BF)
            dk = dk.astype(BF)
            grad_c = grad_c + dot(w, dn_ref[cols, :128])
            grad_k = grad_k + dot(dk, qm[cols])
            acc_q[here, cols] += dot(kth[:, rows], dk)
        dconv_ref[rows] = grad_c.astype(BF)
        acc_k[rows] = grad_k

    @pl.when(h == pl.num_programs(0) - 1)
    def _():
        gq_ref[...] = acc_q[...].T.astype(BF)
        gk_ref[...] = (acc_k[...] + acc_kt[...].T).astype(BF)


def call(body, heads, in_specs, out_specs, out_shape, scratch=()):
    return pl.pallas_call(
        body,
        grid=(heads,),
        in_specs=in_specs,
        out_specs=out_specs,
        out_shape=out_shape,
        scratch_shapes=list(scratch),
        compiler_params=pltpu.CompilerParams(
            dimension_semantics=("arbitrary",), vmem_limit_bytes=LIMIT
        ),
    )


def shifted(block, axis, distance):
    size = lax.axis_size(axis)
    route = [(i - distance, i) for i in range(size) if 0 <= i - distance < size]
    return lax.ppermute(block, axis, route)


def per_device(width, queries, keys, values, conv_weight, gain, cotangent):
    length, channels = values.shape
    heads = queries.shape[1] // FEAT
    feats = heads * FEAT
    blocks = lax.axis_size("ctx")
    margin = CONV - 1
    shape = jax.ShapeDtypeStruct
    col = pl.BlockSpec((length, 128), lambda h: (0, h))
    wide = pl.BlockSpec((length, 256), lambda h: (0, h))
    tok = pl.BlockSpec((length, feats), lambda h: (0, 0))
    feat = pl.BlockSpec((feats, length), lambda h: (0, 0))
    mine = pl.BlockSpec((FEAT, length), lambda h: (h, 0))
    state = pl.BlockSpec((1, ROWS, 256), lambda h: (h, 0, 0))
    gathered = pl.BlockSpec((blocks, 1, ROWS, 256), lambda h: (0, h, 0, 0))
    vec = pl.BlockSpec((1, 128), lambda h: (0, h))
    pad = pl.BlockSpec((length, 128), lambda h: (0, 0))
    smem = pl.BlockSpec(memory_space=pltpu.SMEM)
    index = lax.axis_index("ctx").astype(jnp.int32).reshape(1)
    gain2 = gain.reshape(1, channels)
    previous = shifted(values[length - margin :], "ctx", 1).astype(F32)
    qt, kt = queries.T, keys.T

    conv, local = call(
        state_kernel,
        heads,
        [
            col,
            pl.BlockSpec((margin, 128), lambda h: (0, h)),
            pl.BlockSpec((CONV, 128), lambda h: (0, h)),
            mine,
        ],
        [col, state],
        [shape((length, channels), BF), shape((heads, ROWS, 256), BF)],
    )(values, previous, conv_weight, kt)
    before = lax.all_gather(local, "ctx")

    att, den, stat, prior = call(
        forward_kernel,
        heads,
        [smem, gathered, tok, feat, mine, col, col, vec],
        [col, pad, pl.BlockSpec((8, length), lambda h: (0, 0)), state],
        [
            shape((length, channels), F32),
            shape((length, 128), F32),
            shape((8, length), F32),
            shape((heads, ROWS, 256), BF),
        ],
        [pltpu.VMEM((length, 128), F32)],
    )(index, before, queries, kt, qt, conv, cotangent, gain2)
    stat = lax.psum(stat, "head").T

    normed, dn, back = call(
        functools.partial(norm_kernel, width),
        heads,
        [col, pad, pl.BlockSpec((length, 8), lambda h: (0, 0)), col, vec, mine],
        [col, wide, state],
        [
            shape((length, channels), BF),
            shape((length, heads * 256), BF),
            shape((heads, ROWS, 256), BF),
        ],
    )(att, den, stat, cotangent, gain2, qt)
    after = lax.all_gather(back, "ctx")

    grad_q, grad_k, d_conv = call(
        backward_kernel,
        heads,
        [smem, gathered, tok, tok, feat, mine, mine, col, wide, state],
        [tok, tok, col],
        [
            shape((length, feats), BF),
            shape((length, feats), BF),
            shape((length, channels), BF),
        ],
        [
            pltpu.VMEM((feats, length), F32),
            pltpu.VMEM((feats, length), F32),
            pltpu.VMEM((length, feats), F32),
        ],
    )(index, after, queries, keys, qt, qt, kt, conv, dn, prior)
    following = shifted(d_conv[:margin], "ctx", -1)
    extended = jnp.concatenate([d_conv, following], axis=0)
    total = jnp.zeros(values.shape, F32)
    for tap in range(CONV):
        total = total + conv_weight[tap] * extended[tap : tap + length]
    return (normed, grad_q, grad_k, total.astype(BF))


def solution(mesh):
    two = P("ctx", "head")

    def run(queries, keys, values, conv_weight, gain, cotangent):
        return jax.shard_map(
            functools.partial(per_device, values.shape[1]),
            mesh=mesh,
            in_specs=(two, two, two, P(None, "head"), P("head"), two),
            out_specs=(two, two, two, two),
            check_vma=False,
        )(queries, keys, values, conv_weight, gain, cotangent)

    return run
```

```python
import functools
import math

import jax
import jax.numpy as jnp
from jax import lax
from jax.experimental import pallas as pl
from jax.experimental.pallas import tpu as pltpu
from jax.sharding import PartitionSpec as P

FEAT = 16
CONV = 3
ROWS = 160
TILE = 256
S = 0.25 / math.sqrt(2.0)
EPS = 1e-06
F32 = jnp.float32
BF = jnp.bfloat16
LIMIT = 56 * 1024 * 1024


def dot(a, b):
    return jnp.dot(a, b, preferred_element_type=F32)


def dot_nt(a, b):
    return lax.dot_general(a, b, (((1,), (1,)), ((), ())), preferred_element_type=F32)


def dot_tn(a, b):
    return lax.dot_general(a, b, (((0,), (0,)), ((), ())), preferred_element_type=F32)


def turned(x, d):
    return pltpu.roll(x, FEAT - d, 0)


def phi(x, pair):
    parts = [x * 0.5, (x * x) * S]
    for d in range(1, 8):
        parts.append((x * turned(x, d)) * (pair * S))
    parts.append((x[:8] * x[8:]) * (pair * S))
    row = lax.broadcasted_iota(jnp.int32, (8, x.shape[1]), 0)
    parts.append(jnp.where(row == 0, 1.0, 0.0).astype(F32))
    return jnp.concatenate(parts, axis=0).astype(BF)


def phi_grad(g, x):
    total = g[16:32] * x
    for d in range(1, 8):
        part = g[16 + 16 * d : 32 + 16 * d]
        total = total + part * turned(x, d) + pltpu.roll(part * x, d, 0)
    last = g[144:152]
    total = total + jnp.concatenate([last * x[8:], last * x[:8]], axis=0)
    return g[:16] * 0.5 + (2.0 * S) * total


def lanes(rows):
    return lax.broadcasted_iota(jnp.int32, (rows, 128), 1)


def with_ones(conv):
    ones = jnp.where(lanes(conv.shape[0]) < 2, 1.0, 0.0).astype(BF)
    return jnp.concatenate([conv, ones], axis=1)


def with_split(wide, column, order):
    high = column.astype(BF).astype(F32)
    low = column - high
    lane = lanes(wide.shape[0])
    right = jnp.zeros(lane.shape, F32)
    for at, kind in enumerate(order):
        right = jnp.where(lane == at, high if kind == "h" else low, right)
    return jnp.concatenate([wide.astype(BF), right.astype(BF)], axis=1)


def put_sum(sum_ref, h, column):
    @pl.when(h == 0)
    def _():
        sum_ref[...] = jnp.zeros_like(sum_ref)

    sum_ref[...] = jnp.where(lanes(ROWS) == h, column, sum_ref[...])


def state_kernel(values_ref, prev_ref, taps_ref, kt_ref, conv_ref, state_ref, sum_ref):
    v = values_ref[...].astype(F32)
    row = lax.broadcasted_iota(jnp.int32, v.shape, 0)
    one = jnp.where(row == 0, prev_ref[1:2], pltpu.roll(v, 1, 0))
    two = jnp.where(
        row == 0, prev_ref[0:1], jnp.where(row == 1, prev_ref[1:2], pltpu.roll(v, 2, 0))
    )
    conv = (taps_ref[0:1] * v + taps_ref[1:2] * one + taps_ref[2:3] * two).astype(BF)
    conv_ref[...] = conv
    total = dot(phi(kt_ref[...].astype(F32), 1.0), with_ones(conv))
    state_ref[0] = total[:, :128].astype(BF)
    put_sum(sum_ref, pl.program_id(0), total[:, 128:129])


class Exchange:
    def __init__(self, sign, blocks, state_ref, sum_ref, refs):
        self.sign, self.blocks, self.chips = sign, blocks, blocks // 2
        self.state_ref, self.sum_ref = state_ref, sum_ref
        self.states, self.sums, self.acc, self.give, self.got = refs[:5]
        self.send, self.recv, self.swap_send, self.swap_recv = refs[5:]
        self.me = lax.axis_index("ctx")
        self.chip, self.core = self.me // 2, self.me % 2

    def greet(self, peers=0):
        barrier = pltpu.get_barrier_semaphore()
        for d in range(1, self.chips):
            other = (self.me + 2 * d) % self.blocks
            pl.semaphore_signal(barrier, inc=1, device_id={"ctx": other})
        pl.semaphore_signal(barrier, inc=1, device_id={"ctx": self.me + 1 - 2 * self.core})
        for d in range(1, peers):
            other = (lax.axis_index("head") + d) % peers
            pl.semaphore_signal(barrier, inc=1, device_id={"head": other})
        pl.semaphore_wait(barrier, self.chips + max(peers - 1, 0))

    def copies(self, d):
        to = (self.me + 2 * d * self.sign + self.blocks) % self.blocks
        pairs = [(self.state_ref, self.states), (self.sum_ref, self.sums)]
        return [
            pltpu.make_async_remote_copy(
                src_ref=src,
                dst_ref=dst.at[d - 1],
                send_sem=self.send.at[d - 1, k],
                recv_sem=self.recv.at[d - 1, k],
                device_id={"ctx": to},
            )
            for k, (src, dst) in enumerate(pairs)
        ]

    def swap(self):
        return pltpu.make_async_remote_copy(
            src_ref=self.give,
            dst_ref=self.got,
            send_sem=self.swap_send,
            recv_sem=self.swap_recv,
            device_id={"ctx": self.me + 1 - 2 * self.core},
        )

    def reaches(self, d):
        return self.chip + d < self.chips if self.sign > 0 else self.chip >= d

    def reached(self, d):
        return self.chip >= d if self.sign > 0 else self.chip + d < self.chips

    def start(self):
        for d in range(1, self.chips):

            @pl.when(self.reaches(d))
            def _():
                for copy in self.copies(d):
                    copy.start()

    def merge(self):
        heads = self.state_ref.shape[0]
        self.acc[...] = jnp.zeros_like(self.acc)
        for d in range(1, self.chips):

            @pl.when(self.reached(d))
            def _():
                for copy in self.copies(d):
                    copy.wait_recv()
                self.acc[:heads] += self.states[d - 1].astype(F32)
                self.acc[heads] += self.sums[d - 1]

        self.give[...] = self.acc[...]

        @pl.when(self.core == (0 if self.sign > 0 else 1))
        def _():
            self.give[:heads] += self.state_ref[...].astype(F32)
            self.give[heads] += self.sum_ref[...]

        self.swap().start()

    def finish(self, out, order):
        heads = self.state_ref.shape[0]
        self.swap().wait()
        for d in range(1, self.chips):

            @pl.when(self.reaches(d))
            def _():
                for copy in self.copies(d):
                    copy.wait_send()

        sums = self.acc[heads] + self.got[heads]
        for h in range(heads):
            column = jnp.sum(jnp.where(lanes(ROWS) == h, sums, 0.0), axis=1, keepdims=True)
            out[h] = with_split(self.acc[h] + self.got[h], column, order)


def exchange_scratch(blocks, heads):
    slots = max(blocks // 2 - 1, 1)
    return [
        pltpu.VMEM((slots, heads, ROWS, 128), BF),
        pltpu.VMEM((slots, ROWS, 128), F32),
        pltpu.VMEM((heads + 1, ROWS, 128), F32),
        pltpu.VMEM((heads + 1, ROWS, 128), F32),
        pltpu.VMEM((heads + 1, ROWS, 128), F32),
        pltpu.SemaphoreType.DMA((slots, 2)),
        pltpu.SemaphoreType.DMA((slots, 2)),
        pltpu.SemaphoreType.DMA,
        pltpu.SemaphoreType.DMA,
    ]


def head_rows(ref, h):
    row = lax.broadcasted_iota(jnp.int32, (ref.shape[0], 1), 0)
    return (ref[...].astype(F32) * jnp.where(row // FEAT == h, 1.0, 0.0)).astype(BF)


def head_lanes(ref, h):
    lane = lax.broadcasted_iota(jnp.int32, (1, ref.shape[1]), 1)
    return (ref[...].astype(F32) * jnp.where(lane // FEAT == h, 1.0, 0.0)).astype(BF)


def forward_kernel(
    blocks, peers, heads,
    state_ref, sum_ref, q_ref, kt_ref, qth_ref, conv_ref, cot_ref, gain_ref,
    att_ref, den_ref, stat_ref, prior_ref,
    sums, numer, stat, stats, stat_send, stat_recv, *refs,
):
    step = pl.program_id(0)
    h = step % heads
    exchange = Exchange(1, blocks, state_ref, sum_ref, refs)
    length = conv_ref.shape[0]

    @pl.when(step == 0)
    def _():
        exchange.greet(peers)
        exchange.start()
        sums[...] = jnp.zeros_like(sums)
        den_ref[...] = jnp.zeros_like(den_ref)

    @pl.when(step == heads - 1)
    def _():
        exchange.merge()

    @pl.when(step == heads)
    def _():
        exchange.finish(prior_ref, "hhl")

    @pl.when(step < heads)
    def _():
        kt = head_rows(kt_ref, h)
        conv = with_ones(conv_ref[...])
        causal = lax.broadcasted_iota(jnp.int32, (TILE, TILE), 0) >= lax.broadcasted_iota(
            jnp.int32, (TILE, TILE), 1
        )
        for t0 in range(0, length, TILE):
            q = q_ref[t0 : t0 + TILE]
            d = dot(q, kt[:, t0 : t0 + TILE])
            w = jnp.where(causal, 1.0 + d * (0.25 + d * 0.03125), 0.0).astype(BF)
            out = dot(w, conv[t0 : t0 + TILE])
            if t0:
                d = dot(q, kt[:, :t0])
                w = (1.0 + d * (0.25 + d * 0.03125)).astype(BF)
                out = out + dot(w, conv[:t0])
            numer[h, t0 : t0 + TILE] = out

    @pl.when(step >= heads)
    def _():
        out = numer[h] + dot_tn(phi(qth_ref[...].astype(F32), 2.0), prior_ref[h])
        den = out[:, 128:129] + out[:, 130:131]
        att = out[:, :128] / den
        att_ref[...] = att
        lane = lanes(length)
        den_ref[...] = jnp.where(lane == h, den, den_ref[...])
        square = jnp.sum(att * att, axis=1, keepdims=True)
        agree = jnp.sum(
            att * (cot_ref[...].astype(F32) * gain_ref[...]), axis=1, keepdims=True
        )
        sums[...] += jnp.where(lane == 0, square, jnp.where(lane == 1, agree, 0.0))

    @pl.when(step == 2 * heads - 1)
    def _():
        stat[...] = sums[...].T[:8]
        mine = lax.axis_index("head")
        copies = [
            pltpu.make_async_remote_copy(
                src_ref=stat,
                dst_ref=stats.at[d - 1],
                send_sem=stat_send.at[d - 1],
                recv_sem=stat_recv.at[d - 1],
                device_id={"head": (mine + d) % peers},
            )
            for d in range(1, peers)
        ]
        for copy in copies:
            copy.start()
        total = stat[...]
        for d, copy in enumerate(copies):
            copy.wait()
            total = total + stats[d]
        stat_ref[...] = jnp.concatenate([total] * 16, axis=0).T


def norm_kernel(
    width, att_ref, den_ref, stat_ref, cot_ref, gain_ref, qth_ref, normed_ref, dn_ref, back_ref,
    sum_ref,
):
    h = pl.program_id(0)
    att = att_ref[...]
    gain = gain_ref[...]
    length = att.shape[0]
    den = jnp.sum(jnp.where(lanes(length) == h, den_ref[...], 0.0), axis=1, keepdims=True)
    inv = lax.rsqrt(stat_ref[:, 0:1] / width + EPS)
    shrink = inv * inv * inv * stat_ref[:, 1:2] / width
    normed_ref[...] = (att * inv * gain).astype(BF)
    d_att = inv * (cot_ref[...].astype(F32) * gain) - att * shrink
    each = 1.0 / den
    d_den = -jnp.sum(d_att * att, axis=1, keepdims=True) * each
    dn = with_split(d_att * each, d_den, "hlh")
    dn_ref[...] = dn
    total = dot(phi(qth_ref[...].astype(F32), 1.0), dn)
    back_ref[0] = total[:, :128].astype(BF)
    put_sum(sum_ref, h, total[:, 128:129] + total[:, 129:130])


def backward_kernel(
    blocks, heads,
    state_ref, sum_ref, q_ref, k_ref, qt_ref, qth_ref, kth_ref, conv_ref, dn_ref, prior_ref,
    gq_ref, gk_ref, dconv_ref, acc_q, acc_kt, acc_k, grad_c, later, *refs,
):
    step = pl.program_id(0)
    h = step % heads
    exchange = Exchange(-1, blocks, state_ref, sum_ref, refs)
    length = conv_ref.shape[0]
    here = pl.ds(pl.multiple_of(h * FEAT, FEAT), FEAT)

    @pl.when(step == 0)
    def _():
        exchange.greet()
        exchange.start()
        acc_k[...] = jnp.zeros_like(acc_k)

    @pl.when(step == heads - 1)
    def _():
        exchange.merge()

    @pl.when(step == heads)
    def _():
        exchange.finish(later, "hl")

    @pl.when(step < heads)
    def _():
        conv = with_ones(conv_ref[...])
        qt = head_rows(qt_ref, h)
        qm = head_lanes(q_ref, h)
        kth = kth_ref[...]
        acc_q[here] = phi_grad(dot_nt(prior_ref[0], dn_ref[...]), qth_ref[...].astype(F32))
        causal = lax.broadcasted_iota(jnp.int32, (TILE, TILE), 1) >= lax.broadcasted_iota(
            jnp.int32, (TILE, TILE), 0
        )
        for s0 in range(0, length, TILE):
            rows = slice(s0, s0 + TILE)
            k = k_ref[rows]
            total_c = jnp.zeros((TILE, 128), F32)
            total_k = acc_k[rows]
            pieces = [slice(s0, s0 + TILE)]
            if s0 + TILE < length:
                pieces.append(slice(s0 + TILE, length))
            for at, cols in enumerate(pieces):
                d = dot(k, qt[:, cols])
                w = 1.0 + d * (0.25 + d * 0.03125)
                dk = dot_nt(conv[rows], dn_ref[cols]) * (0.25 + d * 0.0625)
                if at == 0:
                    w = jnp.where(causal, w, 0.0)
                    dk = jnp.where(causal, dk, 0.0)
                w = w.astype(BF)
                dk = dk.astype(BF)
                total_c = total_c + dot(w, dn_ref[cols, :128])
                total_k = total_k + dot(dk, qm[cols])
                acc_q[here, cols] += dot(kth[:, rows], dk)
            grad_c[h, rows] = total_c
            acc_k[rows] = total_k

    @pl.when(step >= heads)
    def _():
        kx = kth_ref[...].astype(F32)
        acc_kt[here] = phi_grad(dot_nt(later[h], with_ones(conv_ref[...])), kx)
        inter = dot_tn(phi(kx, 2.0), later[h, :, :128])
        dconv_ref[...] = (grad_c[h] + inter).astype(BF)

    @pl.when(step == 2 * heads - 1)
    def _():
        gq_ref[...] = acc_q[...].T.astype(BF)
        gk_ref[...] = (acc_k[...] + acc_kt[...].T).astype(BF)


def call(body, steps, in_specs, out_specs, out_shape, scratch=(), collective_id=None):
    remote = {} if collective_id is None else dict(
        collective_id=collective_id, has_side_effects=True
    )
    return pl.pallas_call(
        body,
        grid=(steps,),
        in_specs=in_specs,
        out_specs=out_specs,
        out_shape=out_shape,
        scratch_shapes=list(scratch),
        compiler_params=pltpu.CompilerParams(
            dimension_semantics=("arbitrary",), vmem_limit_bytes=LIMIT, **remote
        ),
    )


def shifted(block, axis, distance):
    size = lax.axis_size(axis)
    route = [(i - distance, i) for i in range(size) if 0 <= i - distance < size]
    return lax.ppermute(block, axis, route)


def per_device(width, queries, keys, values, conv_weight, gain, cotangent):
    length, channels = values.shape
    heads = queries.shape[1] // FEAT
    feats = heads * FEAT
    blocks = lax.axis_size("ctx")
    margin = CONV - 1
    shape = jax.ShapeDtypeStruct
    peers = lax.axis_size("head")
    col = pl.BlockSpec((length, 128), lambda h: (0, h))
    wide = pl.BlockSpec((length, 256), lambda h: (0, h))
    tok = pl.BlockSpec((length, feats), lambda h: (0, 0))
    feat = pl.BlockSpec((feats, length), lambda h: (0, 0))
    mine = pl.BlockSpec((FEAT, length), lambda h: (h, 0))
    state = pl.BlockSpec((1, ROWS, 128), lambda h: (h, 0, 0))
    states = pl.BlockSpec((heads, ROWS, 128), lambda h: (0, 0, 0))
    priors = pl.BlockSpec((heads, ROWS, 256), lambda h: (0, 0, 0))
    sums = pl.BlockSpec((ROWS, 128), lambda h: (0, 0))
    vec = pl.BlockSpec((1, 128), lambda h: (0, h))
    pad = pl.BlockSpec((length, 128), lambda h: (0, 0))

    def early(i):
        return i % heads * (1 - i // heads) + i // heads * (heads - 1)

    def late(i):
        return i // heads * (i % heads)

    gain2 = gain.reshape(1, channels)
    previous = shifted(values[length - margin :], "ctx", 1).astype(F32)
    qt, kt = queries.T, keys.T

    conv, local, local_sum = call(
        state_kernel,
        heads,
        [
            col,
            pl.BlockSpec((margin, 128), lambda h: (0, h)),
            pl.BlockSpec((CONV, 128), lambda h: (0, h)),
            mine,
        ],
        [col, state, sums],
        [
            shape((length, channels), BF),
            shape((heads, ROWS, 128), BF),
            shape((ROWS, 128), F32),
        ],
    )(values, previous, conv_weight, kt)

    att, den, stat, prior = call(
        functools.partial(forward_kernel, blocks, peers, heads),
        2 * heads,
        [
            states,
            sums,
            tok,
            feat,
            pl.BlockSpec((FEAT, length), lambda i: (late(i), 0)),
            pl.BlockSpec((length, 128), lambda i: (0, early(i))),
            pl.BlockSpec((length, 128), lambda i: (0, late(i))),
            pl.BlockSpec((1, 128), lambda i: (0, late(i))),
        ],
        [pl.BlockSpec((length, 128), lambda i: (0, late(i))), pad, pad, priors],
        [
            shape((length, channels), F32),
            shape((length, 128), F32),
            shape((length, 128), F32),
            shape((heads, ROWS, 256), BF),
        ],
        [
            pltpu.VMEM((length, 128), F32),
            pltpu.VMEM((heads, length, 256), F32),
            pltpu.VMEM((8, length), F32),
            pltpu.VMEM((max(peers - 1, 1), 8, length), F32),
            pltpu.SemaphoreType.DMA((max(peers - 1, 1),)),
            pltpu.SemaphoreType.DMA((max(peers - 1, 1),)),
        ]
        + exchange_scratch(blocks, heads),
        0,
    )(local, local_sum, queries, kt, qt, conv, cotangent, gain2)

    normed, dn, back, back_sum = call(
        functools.partial(norm_kernel, width),
        heads,
        [col, pad, pad, col, vec, mine],
        [col, wide, state, sums],
        [
            shape((length, channels), BF),
            shape((length, heads * 256), BF),
            shape((heads, ROWS, 128), BF),
            shape((ROWS, 128), F32),
        ],
    )(att, den, stat, cotangent, gain2, qt)

    grad_q, grad_k, d_conv = call(
        functools.partial(backward_kernel, blocks, heads),
        2 * heads,
        [
            states,
            sums,
            tok,
            tok,
            feat,
            pl.BlockSpec((FEAT, length), lambda i: (early(i), 0)),
            pl.BlockSpec((FEAT, length), lambda i: (i % heads, 0)),
            pl.BlockSpec((length, 128), lambda i: (0, i % heads)),
            pl.BlockSpec((length, 256), lambda i: (0, early(i))),
            pl.BlockSpec((1, ROWS, 256), lambda i: (early(i), 0, 0)),
        ],
        [tok, tok, pl.BlockSpec((length, 128), lambda i: (0, late(i)))],
        [
            shape((length, feats), BF),
            shape((length, feats), BF),
            shape((length, channels), BF),
        ],
        [
            pltpu.VMEM((feats, length), F32),
            pltpu.VMEM((feats, length), F32),
            pltpu.VMEM((length, feats), F32),
            pltpu.VMEM((heads, length, 128), F32),
            pltpu.VMEM((heads, ROWS, 256), BF),
        ]
        + exchange_scratch(blocks, heads),
        1,
    )(back, back_sum, queries, keys, qt, qt, kt, conv, dn, prior)
    following = shifted(d_conv[:margin], "ctx", -1)
    extended = jnp.concatenate([d_conv, following], axis=0)
    total = jnp.zeros(values.shape, F32)
    for tap in range(CONV):
        total = total + conv_weight[tap] * extended[tap : tap + length]
    return (normed, grad_q, grad_k, total.astype(BF))


def solution(mesh):
    two = P("ctx", "head")

    def run(queries, keys, values, conv_weight, gain, cotangent):
        return jax.shard_map(
            functools.partial(per_device, values.shape[1]),
            mesh=mesh,
            in_specs=(two, two, two, P(None, "head"), P("head"), two),
            out_specs=(two, two, two, two),
            check_vma=False,
        )(queries, keys, values, conv_weight, gain, cotangent)

    return run
```

```python
import functools
import math

import jax
import jax.numpy as jnp
from jax import lax
from jax.experimental import pallas as pl
from jax.experimental.pallas import tpu as pltpu
from jax.sharding import PartitionSpec as P

FEAT = 16
CONV = 3
ROWS = 160
TILE = 256
S = 0.25 / math.sqrt(2.0)
EPS = 1e-06
F32 = jnp.float32
BF = jnp.bfloat16
LIMIT = 56 * 1024 * 1024


def dot(a, b):
    return jnp.dot(a, b, preferred_element_type=F32)


def dot_nt(a, b):
    return lax.dot_general(a, b, (((1,), (1,)), ((), ())), preferred_element_type=F32)


def dot_tn(a, b):
    return lax.dot_general(a, b, (((0,), (0,)), ((), ())), preferred_element_type=F32)


def turned(x, d):
    return pltpu.roll(x, FEAT - d, 0)


def phi(x, pair):
    parts = [x * 0.5, (x * x) * S]
    for d in range(1, 8):
        parts.append((x * turned(x, d)) * (pair * S))
    parts.append((x[:8] * x[8:]) * (pair * S))
    row = lax.broadcasted_iota(jnp.int32, (8, x.shape[1]), 0)
    parts.append(jnp.where(row == 0, 1.0, 0.0).astype(F32))
    return jnp.concatenate(parts, axis=0).astype(BF)


def phi_grad(g, x):
    total = g[16:32] * x
    for d in range(1, 8):
        part = g[16 + 16 * d : 32 + 16 * d]
        total = total + part * turned(x, d) + pltpu.roll(part * x, d, 0)
    last = g[144:152]
    total = total + jnp.concatenate([last * x[8:], last * x[:8]], axis=0)
    return g[:16] * 0.5 + (2.0 * S) * total


def lanes(rows):
    return lax.broadcasted_iota(jnp.int32, (rows, 128), 1)


def with_ones(conv):
    ones = jnp.where(lanes(conv.shape[0]) < 2, 1.0, 0.0).astype(BF)
    return jnp.concatenate([conv, ones], axis=1)


def with_split(wide, column, order):
    high = column.astype(BF).astype(F32)
    low = column - high
    lane = lanes(wide.shape[0])
    right = jnp.zeros(lane.shape, F32)
    for at, kind in enumerate(order):
        right = jnp.where(lane == at, high if kind == "h" else low, right)
    return jnp.concatenate([wide.astype(BF), right.astype(BF)], axis=1)


def put_sum(sum_ref, h, column):
    @pl.when(h == 0)
    def _():
        sum_ref[...] = jnp.zeros_like(sum_ref)

    sum_ref[...] = jnp.where(lanes(ROWS) == h, column, sum_ref[...])


def state_kernel(
    values_ref, prev_ref, taps_ref, q_ref, k_ref, conv_ref, state_ref, sum_ref, qt_ref, kt_ref
):
    h = pl.program_id(0)

    @pl.when(h == 0)
    def _():
        qt_ref[...] = q_ref[...].astype(F32).T.astype(BF)
        kt_ref[...] = k_ref[...].astype(F32).T.astype(BF)

    kt = kt_ref[pl.ds(pl.multiple_of(h * FEAT, FEAT), FEAT)]
    v = values_ref[...].astype(F32)
    row = lax.broadcasted_iota(jnp.int32, v.shape, 0)
    one = jnp.where(row == 0, prev_ref[1:2], pltpu.roll(v, 1, 0))
    two = jnp.where(
        row == 0, prev_ref[0:1], jnp.where(row == 1, prev_ref[1:2], pltpu.roll(v, 2, 0))
    )
    conv = (taps_ref[0:1] * v + taps_ref[1:2] * one + taps_ref[2:3] * two).astype(BF)
    conv_ref[...] = conv
    total = dot(phi(kt.astype(F32), 1.0), with_ones(conv))
    state_ref[0] = total[:, :128].astype(BF)
    put_sum(sum_ref, h, total[:, 128:129])


class Exchange:
    def __init__(self, sign, blocks, state_ref, sum_ref, refs):
        self.sign, self.blocks, self.chips = sign, blocks, blocks // 2
        self.state_ref, self.sum_ref = state_ref, sum_ref
        self.states, self.sums, self.small, self.mate, self.pair = refs[:5]
        self.acc, self.give, self.got, self.acc_s, self.give_s, self.got_s = refs[5:11]
        self.send, self.recv, self.near = refs[11:]
        self.half = state_ref.shape[0] // 2
        self.me = lax.axis_index("ctx")
        self.chip, self.core = self.me // 2, self.me % 2
        self.sibling = self.me + 1 - 2 * self.core

    def greet(self, peers=0):
        barrier = pltpu.get_barrier_semaphore()
        for d in range(1, self.chips):
            other = (self.me + 2 * d) % self.blocks
            pl.semaphore_signal(barrier, inc=1, device_id={"ctx": other})
        pl.semaphore_signal(barrier, inc=1, device_id={"ctx": self.me + 1 - 2 * self.core})
        for d in range(1, peers):
            other = (lax.axis_index("head") + d) % peers
            pl.semaphore_signal(barrier, inc=1, device_id={"head": other})
        pl.semaphore_wait(barrier, self.chips + max(peers - 1, 0))

    def copies(self, d):
        to = (self.me + 2 * d * self.sign + self.blocks) % self.blocks
        pairs = [(self.pair, self.states), (self.small, self.sums)]
        return [
            pltpu.make_async_remote_copy(
                src_ref=src,
                dst_ref=dst.at[d - 1],
                send_sem=self.send.at[d - 1, k],
                recv_sem=self.recv.at[d - 1, k],
                device_id={"ctx": to},
            )
            for k, (src, dst) in enumerate(pairs)
        ]

    def beside(self, src, dst, k):
        return pltpu.make_async_remote_copy(
            src_ref=src,
            dst_ref=dst,
            send_sem=self.near.at[2 * k],
            recv_sem=self.near.at[2 * k + 1],
            device_id={"ctx": self.sibling},
        )

    def first(self):
        return self.beside(
            self.state_ref.at[pl.ds((1 - self.core) * self.half, self.half)], self.mate, 0
        )

    def swap(self):
        return [
            self.beside(self.give, self.got, 1),
            self.beside(self.give_s, self.got_s, 2),
        ]

    def own(self):
        return self.state_ref[pl.ds(self.core * self.half, self.half)].astype(F32)

    def reaches(self, d):
        return self.chip + d < self.chips if self.sign > 0 else self.chip >= d

    def reached(self, d):
        return self.chip >= d if self.sign > 0 else self.chip + d < self.chips

    def start(self):
        self.first().start()
        sums = jnp.concatenate([self.sum_ref[...], jnp.zeros((256 - ROWS, 128), F32)], axis=0)
        self.small[...] = sums.T[:8]

    def spread(self):
        self.first().wait()
        self.pair[...] = (self.own() + self.mate[...].astype(F32)).astype(BF)
        for d in range(1, self.chips):

            @pl.when(self.reaches(d))
            def _():
                for copy in self.copies(d):
                    copy.start()

    def merge(self):
        self.acc[...] = jnp.zeros_like(self.acc)
        self.acc_s[...] = jnp.zeros_like(self.acc_s)
        for d in range(1, self.chips):

            @pl.when(self.reached(d))
            def _():
                for copy in self.copies(d):
                    copy.wait_recv()
                self.acc[...] += self.states[d - 1].astype(F32)
                self.acc_s[...] += self.sums[d - 1]

        self.give[...] = self.acc[...]
        self.give_s[...] = self.acc_s[...]
        leads = self.core == (0 if self.sign > 0 else 1)

        @pl.when(leads)
        def _():
            self.give[...] += self.own()
            self.give_s[...] += self.small[...]

        for copy in self.swap():
            copy.start()

        @pl.when(jnp.logical_not(leads))
        def _():
            self.acc[...] += self.mate[...].astype(F32)

    def finish(self, out, order):
        for copy in self.swap():
            copy.wait()
        for d in range(1, self.chips):

            @pl.when(self.reaches(d))
            def _():
                for copy in self.copies(d):
                    copy.wait_send()

        sums = jnp.concatenate([self.acc_s[...] + self.got_s[...]] * 16, axis=0).T[:ROWS]
        for j in range(self.half):
            for h, part in (
                (self.core * self.half + j, self.acc),
                ((1 - self.core) * self.half + j, self.got),
            ):
                column = jnp.sum(jnp.where(lanes(ROWS) == h, sums, 0.0), axis=1, keepdims=True)
                out[h] = with_split(part[j], column, order)


def exchange_scratch(blocks, heads):
    slots = max(blocks // 2 - 1, 1)
    half = heads // 2
    return (
        [
            pltpu.VMEM((slots, half, ROWS, 128), BF),
            pltpu.VMEM((slots, 8, 256), F32),
            pltpu.VMEM((8, 256), F32),
            pltpu.VMEM((half, ROWS, 128), BF),
            pltpu.VMEM((half, ROWS, 128), BF),
        ]
        + [pltpu.VMEM((half, ROWS, 128), F32)] * 3
        + [pltpu.VMEM((8, 256), F32)] * 3
        + [
            pltpu.SemaphoreType.DMA((slots, 2)),
            pltpu.SemaphoreType.DMA((slots, 2)),
            pltpu.SemaphoreType.DMA((6,)),
        ]
    )


def head_rows(ref, h):
    row = lax.broadcasted_iota(jnp.int32, (ref.shape[0], 1), 0)
    return (ref[...].astype(F32) * jnp.where(row // FEAT == h, 1.0, 0.0)).astype(BF)


def head_lanes(ref, h):
    lane = lax.broadcasted_iota(jnp.int32, (1, ref.shape[1]), 1)
    return (ref[...].astype(F32) * jnp.where(lane // FEAT == h, 1.0, 0.0)).astype(BF)


def forward_kernel(
    blocks, peers, heads,
    state_ref, sum_ref, q_ref, kt_ref, qth_ref, conv_ref, cot_ref, gain_ref,
    att_ref, den_ref, stat_ref, prior_ref,
    sums, numer, stat, stats, stat_send, stat_recv, *refs,
):
    step = pl.program_id(0)
    h = step % heads
    exchange = Exchange(1, blocks, state_ref, sum_ref, refs)
    length = conv_ref.shape[0]

    @pl.when(step == 0)
    def _():
        exchange.greet(peers)
        exchange.start()
        sums[...] = jnp.zeros_like(sums)
        den_ref[...] = jnp.zeros_like(den_ref)

    @pl.when(step == 1)
    def _():
        exchange.spread()

    @pl.when(step == heads - 1)
    def _():
        exchange.merge()

    @pl.when(step == heads)
    def _():
        exchange.finish(prior_ref, "hhl")

    @pl.when(step < heads)
    def _():
        kt = head_rows(kt_ref, h)
        conv = with_ones(conv_ref[...])
        causal = lax.broadcasted_iota(jnp.int32, (TILE, TILE), 0) >= lax.broadcasted_iota(
            jnp.int32, (TILE, TILE), 1
        )
        for t0 in range(0, length, TILE):
            q = q_ref[t0 : t0 + TILE]
            d = dot(q, kt[:, t0 : t0 + TILE])
            w = jnp.where(causal, 1.0 + d * (0.25 + d * 0.03125), 0.0).astype(BF)
            out = dot(w, conv[t0 : t0 + TILE])
            if t0:
                d = dot(q, kt[:, :t0])
                w = (1.0 + d * (0.25 + d * 0.03125)).astype(BF)
                out = out + dot(w, conv[:t0])
            numer[h, t0 : t0 + TILE] = out

    @pl.when(step >= heads)
    def _():
        out = numer[h] + dot_tn(phi(qth_ref[...].astype(F32), 2.0), prior_ref[h])
        den = out[:, 128:129] + out[:, 130:131]
        att = out[:, :128] / den
        att_ref[...] = att
        lane = lanes(length)
        den_ref[...] = jnp.where(lane == h, den, den_ref[...])
        square = jnp.sum(att * att, axis=1, keepdims=True)
        agree = jnp.sum(
            att * (cot_ref[...].astype(F32) * gain_ref[...]), axis=1, keepdims=True
        )
        sums[...] += jnp.where(lane == 0, square, jnp.where(lane == 1, agree, 0.0))

    @pl.when(step == 2 * heads - 1)
    def _():
        stat[...] = sums[...].T[:8]
        mine = lax.axis_index("head")
        copies = [
            pltpu.make_async_remote_copy(
                src_ref=stat,
                dst_ref=stats.at[d - 1],
                send_sem=stat_send.at[d - 1],
                recv_sem=stat_recv.at[d - 1],
                device_id={"head": (mine + d) % peers},
            )
            for d in range(1, peers)
        ]
        for copy in copies:
            copy.start()
        total = stat[...]
        for d, copy in enumerate(copies):
            copy.wait()
            total = total + stats[d]
        stat_ref[...] = jnp.concatenate([total] * 16, axis=0).T


def norm_kernel(
    width, att_ref, den_ref, stat_ref, cot_ref, gain_ref, qth_ref, normed_ref, dn_ref, back_ref,
    sum_ref,
):
    h = pl.program_id(0)
    att = att_ref[...]
    gain = gain_ref[...]
    length = att.shape[0]
    den = jnp.sum(jnp.where(lanes(length) == h, den_ref[...], 0.0), axis=1, keepdims=True)
    inv = lax.rsqrt(stat_ref[:, 0:1] / width + EPS)
    shrink = inv * inv * inv * stat_ref[:, 1:2] / width
    normed_ref[...] = (att * inv * gain).astype(BF)
    d_att = inv * (cot_ref[...].astype(F32) * gain) - att * shrink
    each = 1.0 / den
    d_den = -jnp.sum(d_att * att, axis=1, keepdims=True) * each
    dn = with_split(d_att * each, d_den, "hlh")
    dn_ref[...] = dn
    total = dot(phi(qth_ref[...].astype(F32), 1.0), dn)
    back_ref[0] = total[:, :128].astype(BF)
    put_sum(sum_ref, h, total[:, 128:129] + total[:, 129:130])


def backward_kernel(
    blocks, heads,
    state_ref, sum_ref, q_ref, k_ref, qt_ref, qth_ref, kth_ref, conv_ref, dn_ref, prior_ref,
    gq_ref, gk_ref, dconv_ref, acc_q, acc_kt, acc_k, grad_c, later, *refs,
):
    step = pl.program_id(0)
    h = step % heads
    exchange = Exchange(-1, blocks, state_ref, sum_ref, refs)
    length = conv_ref.shape[0]
    here = pl.ds(pl.multiple_of(h * FEAT, FEAT), FEAT)

    @pl.when(step == 0)
    def _():
        exchange.greet()
        exchange.start()
        acc_k[...] = jnp.zeros_like(acc_k)

    @pl.when(step == 1)
    def _():
        exchange.spread()

    @pl.when(step == heads - 1)
    def _():
        exchange.merge()

    @pl.when(step == heads)
    def _():
        exchange.finish(later, "hl")

    @pl.when(step < heads)
    def _():
        conv = with_ones(conv_ref[...])
        qt = head_rows(qt_ref, h)
        qm = head_lanes(q_ref, h)
        kth = kth_ref[...]
        acc_q[here] = phi_grad(dot_nt(prior_ref[0], dn_ref[...]), qth_ref[...].astype(F32))
        causal = lax.broadcasted_iota(jnp.int32, (TILE, TILE), 1) >= lax.broadcasted_iota(
            jnp.int32, (TILE, TILE), 0
        )
        for s0 in range(0, length, TILE):
            rows = slice(s0, s0 + TILE)
            k = k_ref[rows]
            total_c = jnp.zeros((TILE, 128), F32)
            total_k = acc_k[rows]
            pieces = [slice(s0, s0 + TILE)]
            if s0 + TILE < length:
                pieces.append(slice(s0 + TILE, length))
            for at, cols in enumerate(pieces):
                d = dot(k, qt[:, cols])
                w = 1.0 + d * (0.25 + d * 0.03125)
                dk = dot_nt(conv[rows], dn_ref[cols]) * (0.25 + d * 0.0625)
                if at == 0:
                    w = jnp.where(causal, w, 0.0)
                    dk = jnp.where(causal, dk, 0.0)
                w = w.astype(BF)
                dk = dk.astype(BF)
                total_c = total_c + dot(w, dn_ref[cols, :128])
                total_k = total_k + dot(dk, qm[cols])
                acc_q[here, cols] += dot(kth[:, rows], dk)
            grad_c[h, rows] = total_c
            acc_k[rows] = total_k

    @pl.when(step >= heads)
    def _():
        kx = kth_ref[...].astype(F32)
        acc_kt[here] = phi_grad(dot_nt(later[h], with_ones(conv_ref[...])), kx)
        inter = dot_tn(phi(kx, 2.0), later[h, :, :128])
        dconv_ref[...] = (grad_c[h] + inter).astype(BF)

    @pl.when(step == 2 * heads - 1)
    def _():
        gq_ref[...] = acc_q[...].T.astype(BF)
        gk_ref[...] = (acc_k[...] + acc_kt[...].T).astype(BF)


def call(body, steps, in_specs, out_specs, out_shape, scratch=(), collective_id=None):
    remote = {} if collective_id is None else dict(
        collective_id=collective_id, has_side_effects=True
    )
    return pl.pallas_call(
        body,
        grid=(steps,),
        in_specs=in_specs,
        out_specs=out_specs,
        out_shape=out_shape,
        scratch_shapes=list(scratch),
        compiler_params=pltpu.CompilerParams(
            dimension_semantics=("arbitrary",), vmem_limit_bytes=LIMIT, **remote
        ),
    )


def shifted(block, axis, distance):
    size = lax.axis_size(axis)
    route = [(i - distance, i) for i in range(size) if 0 <= i - distance < size]
    return lax.ppermute(block, axis, route)


def per_device(width, queries, keys, values, conv_weight, gain, cotangent):
    length, channels = values.shape
    heads = queries.shape[1] // FEAT
    feats = heads * FEAT
    blocks = lax.axis_size("ctx")
    margin = CONV - 1
    shape = jax.ShapeDtypeStruct
    peers = lax.axis_size("head")
    col = pl.BlockSpec((length, 128), lambda h: (0, h))
    wide = pl.BlockSpec((length, 256), lambda h: (0, h))
    tok = pl.BlockSpec((length, feats), lambda h: (0, 0))
    feat = pl.BlockSpec((feats, length), lambda h: (0, 0))
    mine = pl.BlockSpec((FEAT, length), lambda h: (h, 0))
    state = pl.BlockSpec((1, ROWS, 128), lambda h: (h, 0, 0))
    states = pl.BlockSpec((heads, ROWS, 128), lambda h: (0, 0, 0))
    priors = pl.BlockSpec((heads, ROWS, 256), lambda h: (0, 0, 0))
    sums = pl.BlockSpec((ROWS, 128), lambda h: (0, 0))
    vec = pl.BlockSpec((1, 128), lambda h: (0, h))
    pad = pl.BlockSpec((length, 128), lambda h: (0, 0))

    def early(i):
        return i % heads * (1 - i // heads) + i // heads * (heads - 1)

    def late(i):
        return i // heads * (i % heads)

    gain2 = gain.reshape(1, channels)
    previous = shifted(values[length - margin :], "ctx", 1).astype(F32)

    conv, local, local_sum, qt, kt = call(
        state_kernel,
        heads,
        [
            col,
            pl.BlockSpec((margin, 128), lambda h: (0, h)),
            pl.BlockSpec((CONV, 128), lambda h: (0, h)),
            tok,
            tok,
        ],
        [col, state, sums, feat, feat],
        [
            shape((length, channels), BF),
            shape((heads, ROWS, 128), BF),
            shape((ROWS, 128), F32),
            shape((feats, length), BF),
            shape((feats, length), BF),
        ],
    )(values, previous, conv_weight, queries, keys)

    att, den, stat, prior = call(
        functools.partial(forward_kernel, blocks, peers, heads),
        2 * heads,
        [
            states,
            sums,
            tok,
            feat,
            pl.BlockSpec((FEAT, length), lambda i: (late(i), 0)),
            pl.BlockSpec((length, 128), lambda i: (0, early(i))),
            pl.BlockSpec((length, 128), lambda i: (0, late(i))),
            pl.BlockSpec((1, 128), lambda i: (0, late(i))),
        ],
        [pl.BlockSpec((length, 128), lambda i: (0, late(i))), pad, pad, priors],
        [
            shape((length, channels), F32),
            shape((length, 128), F32),
            shape((length, 128), F32),
            shape((heads, ROWS, 256), BF),
        ],
        [
            pltpu.VMEM((length, 128), F32),
            pltpu.VMEM((heads, length, 256), F32),
            pltpu.VMEM((8, length), F32),
            pltpu.VMEM((max(peers - 1, 1), 8, length), F32),
            pltpu.SemaphoreType.DMA((max(peers - 1, 1),)),
            pltpu.SemaphoreType.DMA((max(peers - 1, 1),)),
        ]
        + exchange_scratch(blocks, heads),
        0,
    )(local, local_sum, queries, kt, qt, conv, cotangent, gain2)

    normed, dn, back, back_sum = call(
        functools.partial(norm_kernel, width),
        heads,
        [col, pad, pad, col, vec, mine],
        [col, wide, state, sums],
        [
            shape((length, channels), BF),
            shape((length, heads * 256), BF),
            shape((heads, ROWS, 128), BF),
            shape((ROWS, 128), F32),
        ],
    )(att, den, stat, cotangent, gain2, qt)

    grad_q, grad_k, d_conv = call(
        functools.partial(backward_kernel, blocks, heads),
        2 * heads,
        [
            states,
            sums,
            tok,
            tok,
            feat,
            pl.BlockSpec((FEAT, length), lambda i: (early(i), 0)),
            pl.BlockSpec((FEAT, length), lambda i: (i % heads, 0)),
            pl.BlockSpec((length, 128), lambda i: (0, i % heads)),
            pl.BlockSpec((length, 256), lambda i: (0, early(i))),
            pl.BlockSpec((1, ROWS, 256), lambda i: (early(i), 0, 0)),
        ],
        [tok, tok, pl.BlockSpec((length, 128), lambda i: (0, late(i)))],
        [
            shape((length, feats), BF),
            shape((length, feats), BF),
            shape((length, channels), BF),
        ],
        [
            pltpu.VMEM((feats, length), F32),
            pltpu.VMEM((feats, length), F32),
            pltpu.VMEM((length, feats), F32),
            pltpu.VMEM((heads, length, 128), F32),
            pltpu.VMEM((heads, ROWS, 256), BF),
        ]
        + exchange_scratch(blocks, heads),
        1,
    )(back, back_sum, queries, keys, qt, qt, kt, conv, dn, prior)
    following = shifted(d_conv[:margin], "ctx", -1)
    extended = jnp.concatenate([d_conv, following], axis=0)
    total = jnp.zeros(values.shape, F32)
    for tap in range(CONV):
        total = total + conv_weight[tap] * extended[tap : tap + length]
    return (normed, grad_q, grad_k, total.astype(BF))


def solution(mesh):
    two = P("ctx", "head")

    def run(queries, keys, values, conv_weight, gain, cotangent):
        return jax.shard_map(
            functools.partial(per_device, values.shape[1]),
            mesh=mesh,
            in_specs=(two, two, two, P(None, "head"), P("head"), two),
            out_specs=(two, two, two, two),
            check_vma=False,
        )(queries, keys, values, conv_weight, gain, cotangent)

    return run
```

```python
import functools
import math

import jax
import jax.numpy as jnp
from jax import lax
from jax.experimental import pallas as pl
from jax.experimental.pallas import tpu as pltpu
from jax.sharding import PartitionSpec as P

FEAT = 16
CONV = 3
ROWS = 160
EDGE = 16
TILE = 256
S = 0.25 / math.sqrt(2.0)
EPS = 1e-06
F32 = jnp.float32
BF = jnp.bfloat16
LIMIT = 56 * 1024 * 1024


def dot(a, b):
    return jnp.dot(a, b, preferred_element_type=F32)


def dot_nt(a, b):
    return lax.dot_general(a, b, (((1,), (1,)), ((), ())), preferred_element_type=F32)


def dot_tn(a, b):
    return lax.dot_general(a, b, (((0,), (0,)), ((), ())), preferred_element_type=F32)


def turned(x, d):
    return pltpu.roll(x, FEAT - d, 0)


def phi(x, pair):
    parts = [x * 0.5, (x * x) * S]
    for d in range(1, 8):
        parts.append((x * turned(x, d)) * (pair * S))
    parts.append((x[:8] * x[8:]) * (pair * S))
    row = lax.broadcasted_iota(jnp.int32, (8, x.shape[1]), 0)
    parts.append(jnp.where(row == 0, 1.0, 0.0).astype(F32))
    return jnp.concatenate(parts, axis=0).astype(BF)


def phi_grad(g, x):
    total = g[16:32] * x
    for d in range(1, 8):
        part = g[16 + 16 * d : 32 + 16 * d]
        total = total + part * turned(x, d) + pltpu.roll(part * x, d, 0)
    last = g[144:152]
    total = total + jnp.concatenate([last * x[8:], last * x[:8]], axis=0)
    return g[:16] * 0.5 + (2.0 * S) * total


def lanes(rows):
    return lax.broadcasted_iota(jnp.int32, (rows, 128), 1)


def with_ones(conv):
    ones = jnp.where(lanes(conv.shape[0]) < 2, 1.0, 0.0).astype(BF)
    return jnp.concatenate([conv, ones], axis=1)


def with_split(wide, column, order):
    high = column.astype(BF).astype(F32)
    low = column - high
    lane = lanes(wide.shape[0])
    right = jnp.zeros(lane.shape, F32)
    for at, kind in enumerate(order):
        right = jnp.where(lane == at, high if kind == "h" else low, right)
    return jnp.concatenate([wide.astype(BF), right.astype(BF)], axis=1)


def put_sum(sum_ref, h, column):
    @pl.when(h == 0)
    def _():
        sum_ref[...] = jnp.zeros_like(sum_ref)

    sum_ref[...] = jnp.where(lanes(ROWS) == h, column, sum_ref[...])


def state_kernel(
    blocks, values_all, values_ref, taps_ref, q_ref, k_ref,
    conv_ref, state_ref, sum_ref, qt_ref, kt_ref, halo, send, recv,
):
    h = pl.program_id(0)
    me = lax.axis_index("ctx")
    copy = pltpu.make_async_remote_copy(
        src_ref=values_all.at[pl.ds(values_ref.shape[0] - EDGE, EDGE)],
        dst_ref=halo,
        send_sem=send,
        recv_sem=recv,
        device_id={"ctx": (me + 1) % blocks},
    )

    @pl.when(h == 0)
    def _():
        barrier = pltpu.get_barrier_semaphore()

        @pl.when(me > 0)
        def _():
            pl.semaphore_signal(
                barrier, inc=1, device_id={"ctx": (me + blocks - 1) % blocks}
            )

        @pl.when(me + 1 < blocks)
        def _():
            pl.semaphore_wait(barrier, 1)
            copy.start()

        qt_ref[...] = q_ref[...].astype(F32).T.astype(BF)
        kt_ref[...] = k_ref[...].astype(F32).T.astype(BF)

        @pl.when(me > 0)
        def _():
            copy.wait_recv()

        @pl.when(me == 0)
        def _():
            halo[...] = jnp.zeros_like(halo)

        @pl.when(me + 1 < blocks)
        def _():
            copy.wait_send()

    prev = halo[:, pl.ds(pl.multiple_of(h * 128, 128), 128)].astype(F32)

    kt = kt_ref[pl.ds(pl.multiple_of(h * FEAT, FEAT), FEAT)]
    v = values_ref[...].astype(F32)
    row = lax.broadcasted_iota(jnp.int32, v.shape, 0)
    one = jnp.where(row == 0, prev[EDGE - 1 :], pltpu.roll(v, 1, 0))
    two = jnp.where(
        row == 0, prev[EDGE - 2 : EDGE - 1], jnp.where(row == 1, prev[EDGE - 1 :], pltpu.roll(v, 2, 0))
    )
    conv = (taps_ref[0:1] * v + taps_ref[1:2] * one + taps_ref[2:3] * two).astype(BF)
    conv_ref[...] = conv
    total = dot(phi(kt.astype(F32), 1.0), with_ones(conv))
    state_ref[0] = total[:, :128].astype(BF)
    put_sum(sum_ref, h, total[:, 128:129])


class Exchange:
    def __init__(self, sign, blocks, state_ref, sum_ref, refs):
        self.sign, self.blocks, self.chips = sign, blocks, blocks // 2
        self.state_ref, self.sum_ref = state_ref, sum_ref
        self.states, self.sums, self.small, self.mate, self.pair = refs[:5]
        self.acc, self.give, self.got, self.acc_s, self.give_s, self.got_s = refs[5:11]
        self.send, self.recv, self.near = refs[11:]
        self.half = state_ref.shape[0] // 2
        self.me = lax.axis_index("ctx")
        self.chip, self.core = self.me // 2, self.me % 2
        self.sibling = self.me + 1 - 2 * self.core

    def greet(self, peers=0, edge=False):
        barrier = pltpu.get_barrier_semaphore()
        for d in range(1, self.chips):
            other = (self.me + 2 * d) % self.blocks
            pl.semaphore_signal(barrier, inc=1, device_id={"ctx": other})
        pl.semaphore_signal(barrier, inc=1, device_id={"ctx": self.me + 1 - 2 * self.core})
        for d in range(1, peers):
            other = (lax.axis_index("head") + d) % peers
            pl.semaphore_signal(barrier, inc=1, device_id={"head": other})
        if edge:

            @pl.when(self.me + 1 < self.blocks)
            def _():
                other = (self.me + 1) % self.blocks
                pl.semaphore_signal(barrier, inc=1, device_id={"ctx": other})

        number = self.chips + max(peers - 1, 0)
        if edge:
            number = number + jnp.where(self.me > 0, 1, 0)
        pl.semaphore_wait(barrier, number)

    def copies(self, d):
        to = (self.me + 2 * d * self.sign + self.blocks) % self.blocks
        pairs = [(self.pair, self.states), (self.small, self.sums)]
        return [
            pltpu.make_async_remote_copy(
                src_ref=src,
                dst_ref=dst.at[d - 1],
                send_sem=self.send.at[d - 1, k],
                recv_sem=self.recv.at[d - 1, k],
                device_id={"ctx": to},
            )
            for k, (src, dst) in enumerate(pairs)
        ]

    def beside(self, src, dst, k):
        return pltpu.make_async_remote_copy(
            src_ref=src,
            dst_ref=dst,
            send_sem=self.near.at[2 * k],
            recv_sem=self.near.at[2 * k + 1],
            device_id={"ctx": self.sibling},
        )

    def first(self):
        return self.beside(
            self.state_ref.at[pl.ds((1 - self.core) * self.half, self.half)], self.mate, 0
        )

    def swap(self):
        return [
            self.beside(self.give, self.got, 1),
            self.beside(self.give_s, self.got_s, 2),
        ]

    def own(self):
        return self.state_ref[pl.ds(self.core * self.half, self.half)].astype(F32)

    def reaches(self, d):
        return self.chip + d < self.chips if self.sign > 0 else self.chip >= d

    def reached(self, d):
        return self.chip >= d if self.sign > 0 else self.chip + d < self.chips

    def start(self):
        self.first().start()
        sums = jnp.concatenate([self.sum_ref[...], jnp.zeros((256 - ROWS, 128), F32)], axis=0)
        self.small[...] = sums.T[:8]

    def spread(self):
        self.first().wait()
        self.pair[...] = (self.own() + self.mate[...].astype(F32)).astype(BF)
        for d in range(1, self.chips):

            @pl.when(self.reaches(d))
            def _():
                for copy in self.copies(d):
                    copy.start()

    def merge(self):
        self.acc[...] = jnp.zeros_like(self.acc)
        self.acc_s[...] = jnp.zeros_like(self.acc_s)
        for d in range(1, self.chips):

            @pl.when(self.reached(d))
            def _():
                for copy in self.copies(d):
                    copy.wait_recv()
                self.acc[...] += self.states[d - 1].astype(F32)
                self.acc_s[...] += self.sums[d - 1]

        self.give[...] = self.acc[...]
        self.give_s[...] = self.acc_s[...]
        leads = self.core == (0 if self.sign > 0 else 1)

        @pl.when(leads)
        def _():
            self.give[...] += self.own()
            self.give_s[...] += self.small[...]

        for copy in self.swap():
            copy.start()

        @pl.when(jnp.logical_not(leads))
        def _():
            self.acc[...] += self.mate[...].astype(F32)

    def finish(self, out, order):
        for copy in self.swap():
            copy.wait()
        for d in range(1, self.chips):

            @pl.when(self.reaches(d))
            def _():
                for copy in self.copies(d):
                    copy.wait_send()

        sums = jnp.concatenate([self.acc_s[...] + self.got_s[...]] * 16, axis=0).T[:ROWS]
        for j in range(self.half):
            for h, part in (
                (self.core * self.half + j, self.acc),
                ((1 - self.core) * self.half + j, self.got),
            ):
                column = jnp.sum(jnp.where(lanes(ROWS) == h, sums, 0.0), axis=1, keepdims=True)
                out[h] = with_split(part[j], column, order)


def exchange_scratch(blocks, heads):
    slots = max(blocks // 2 - 1, 1)
    half = heads // 2
    return (
        [
            pltpu.VMEM((slots, half, ROWS, 128), BF),
            pltpu.VMEM((slots, 8, 256), F32),
            pltpu.VMEM((8, 256), F32),
            pltpu.VMEM((half, ROWS, 128), BF),
            pltpu.VMEM((half, ROWS, 128), BF),
        ]
        + [pltpu.VMEM((half, ROWS, 128), F32)] * 3
        + [pltpu.VMEM((8, 256), F32)] * 3
        + [
            pltpu.SemaphoreType.DMA((slots, 2)),
            pltpu.SemaphoreType.DMA((slots, 2)),
            pltpu.SemaphoreType.DMA((6,)),
        ]
    )


def head_rows(ref, h):
    row = lax.broadcasted_iota(jnp.int32, (ref.shape[0], 1), 0)
    return (ref[...].astype(F32) * jnp.where(row // FEAT == h, 1.0, 0.0)).astype(BF)


def head_lanes(ref, h):
    lane = lax.broadcasted_iota(jnp.int32, (1, ref.shape[1]), 1)
    return (ref[...].astype(F32) * jnp.where(lane // FEAT == h, 1.0, 0.0)).astype(BF)


def forward_kernel(
    blocks, peers, heads,
    state_ref, sum_ref, q_ref, kt_ref, qth_ref, conv_ref, cot_ref, gain_ref,
    att_ref, den_ref, stat_ref, prior_ref,
    sums, numer, stat, stats, stat_send, stat_recv, *refs,
):
    step = pl.program_id(0)
    h = step % heads
    exchange = Exchange(1, blocks, state_ref, sum_ref, refs)
    length = conv_ref.shape[0]

    @pl.when(step == 0)
    def _():
        exchange.greet(peers)
        exchange.start()
        sums[...] = jnp.zeros_like(sums)
        den_ref[...] = jnp.zeros_like(den_ref)

    @pl.when(step == 1)
    def _():
        exchange.spread()

    @pl.when(step == heads - 1)
    def _():
        exchange.merge()

    @pl.when(step == heads)
    def _():
        exchange.finish(prior_ref, "hhl")

    @pl.when(step < heads)
    def _():
        kt = head_rows(kt_ref, h)
        conv = with_ones(conv_ref[...])
        causal = lax.broadcasted_iota(jnp.int32, (TILE, TILE), 0) >= lax.broadcasted_iota(
            jnp.int32, (TILE, TILE), 1
        )
        for t0 in range(0, length, TILE):
            q = q_ref[t0 : t0 + TILE]
            d = dot(q, kt[:, t0 : t0 + TILE])
            w = jnp.where(causal, 1.0 + d * (0.25 + d * 0.03125), 0.0).astype(BF)
            out = dot(w, conv[t0 : t0 + TILE])
            if t0:
                d = dot(q, kt[:, :t0])
                w = (1.0 + d * (0.25 + d * 0.03125)).astype(BF)
                out = out + dot(w, conv[:t0])
            numer[h, t0 : t0 + TILE] = out

    @pl.when(step >= heads)
    def _():
        out = numer[h] + dot_tn(phi(qth_ref[...].astype(F32), 2.0), prior_ref[h])
        den = out[:, 128:129] + out[:, 130:131]
        att = out[:, :128] / den
        att_ref[...] = att
        lane = lanes(length)
        den_ref[...] = jnp.where(lane == h, den, den_ref[...])
        square = jnp.sum(att * att, axis=1, keepdims=True)
        agree = jnp.sum(
            att * (cot_ref[...].astype(F32) * gain_ref[...]), axis=1, keepdims=True
        )
        sums[...] += jnp.where(lane == 0, square, jnp.where(lane == 1, agree, 0.0))

    @pl.when(step == 2 * heads - 1)
    def _():
        stat[...] = sums[...].T[:8]
        mine = lax.axis_index("head")
        copies = [
            pltpu.make_async_remote_copy(
                src_ref=stat,
                dst_ref=stats.at[d - 1],
                send_sem=stat_send.at[d - 1],
                recv_sem=stat_recv.at[d - 1],
                device_id={"head": (mine + d) % peers},
            )
            for d in range(1, peers)
        ]
        for copy in copies:
            copy.start()
        total = stat[...]
        for d, copy in enumerate(copies):
            copy.wait()
            total = total + stats[d]
        stat_ref[...] = jnp.concatenate([total] * 16, axis=0).T


def norm_kernel(
    width, att_ref, den_ref, stat_ref, cot_ref, gain_ref, qth_ref, normed_ref, dn_ref, back_ref,
    sum_ref,
):
    h = pl.program_id(0)
    att = att_ref[...]
    gain = gain_ref[...]
    length = att.shape[0]
    den = jnp.sum(jnp.where(lanes(length) == h, den_ref[...], 0.0), axis=1, keepdims=True)
    inv = lax.rsqrt(stat_ref[:, 0:1] / width + EPS)
    shrink = inv * inv * inv * stat_ref[:, 1:2] / width
    normed_ref[...] = (att * inv * gain).astype(BF)
    d_att = inv * (cot_ref[...].astype(F32) * gain) - att * shrink
    each = 1.0 / den
    d_den = -jnp.sum(d_att * att, axis=1, keepdims=True) * each
    dn = with_split(d_att * each, d_den, "hlh")
    dn_ref[...] = dn
    total = dot(phi(qth_ref[...].astype(F32), 1.0), dn)
    back_ref[0] = total[:, :128].astype(BF)
    put_sum(sum_ref, h, total[:, 128:129] + total[:, 129:130])


def back_conv(x, taps):
    n = x.shape[0]
    total = taps[0:1] * x + taps[1:2] * pltpu.roll(x, n - 1, 0)
    return (total + taps[2:3] * pltpu.roll(x, n - 2, 0)).astype(BF)


def backward_kernel(
    blocks, heads,
    state_ref, sum_ref, q_ref, k_ref, qt_ref, qth_ref, kth_ref, conv_ref, dn_ref, prior_ref,
    taps_ref, gq_ref, gk_ref, gv_ref, acc_q, acc_kt, acc_k, grad_c, later,
    head, tail, after, edge_send, edge_recv, *refs,
):
    step = pl.program_id(0)
    h = step % heads
    exchange = Exchange(-1, blocks, state_ref, sum_ref, refs)
    length = conv_ref.shape[0]
    here = pl.ds(pl.multiple_of(h * FEAT, FEAT), FEAT)

    @pl.when(step == 0)
    def _():
        exchange.greet(edge=True)
        exchange.start()
        acc_k[...] = jnp.zeros_like(acc_k)

    @pl.when(step == 1)
    def _():
        exchange.spread()

    @pl.when(step == heads - 1)
    def _():
        exchange.merge()

    @pl.when(step == heads)
    def _():
        exchange.finish(later, "hl")

    @pl.when(step < heads)
    def _():
        conv = with_ones(conv_ref[...])
        qt = head_rows(qt_ref, h)
        qm = head_lanes(q_ref, h)
        kth = kth_ref[...]
        acc_q[here] = phi_grad(dot_nt(prior_ref[0], dn_ref[...]), qth_ref[...].astype(F32))
        causal = lax.broadcasted_iota(jnp.int32, (TILE, TILE), 1) >= lax.broadcasted_iota(
            jnp.int32, (TILE, TILE), 0
        )
        for s0 in range(0, length, TILE):
            rows = slice(s0, s0 + TILE)
            k = k_ref[rows]
            total_c = jnp.zeros((TILE, 128), F32)
            total_k = acc_k[rows]
            pieces = [slice(s0, s0 + TILE)]
            if s0 + TILE < length:
                pieces.append(slice(s0 + TILE, length))
            for at, cols in enumerate(pieces):
                d = dot(k, qt[:, cols])
                w = 1.0 + d * (0.25 + d * 0.03125)
                dk = dot_nt(conv[rows], dn_ref[cols]) * (0.25 + d * 0.0625)
                if at == 0:
                    w = jnp.where(causal, w, 0.0)
                    dk = jnp.where(causal, dk, 0.0)
                w = w.astype(BF)
                dk = dk.astype(BF)
                total_c = total_c + dot(w, dn_ref[cols, :128])
                total_k = total_k + dot(dk, qm[cols])
                acc_q[here, cols] += dot(kth[:, rows], dk)
            grad_c[h, rows] = total_c
            acc_k[rows] = total_k

    @pl.when(step >= heads)
    def _():
        kx = kth_ref[...].astype(F32)
        acc_kt[here] = phi_grad(dot_nt(later[h], with_ones(conv_ref[...])), kx)
        inter = dot_tn(phi(kx, 2.0), later[h, :, :128])
        d_conv = (grad_c[h] + inter).astype(BF)
        cols = pl.ds(pl.multiple_of(h * 128, 128), 128)
        head[:, cols] = d_conv[:EDGE]
        tail[:, cols] = d_conv[length - EDGE :]
        gv_ref[:, cols] = back_conv(d_conv.astype(F32), taps_ref[:, cols])

    @pl.when(step == 2 * heads - 1)
    def _():
        me = exchange.me
        copy = pltpu.make_async_remote_copy(
            src_ref=head,
            dst_ref=after,
            send_sem=edge_send,
            recv_sem=edge_recv,
            device_id={"ctx": (me + blocks - 1) % blocks},
        )

        @pl.when(me > 0)
        def _():
            copy.start()

        gq_ref[...] = acc_q[...].T.astype(BF)
        gk_ref[...] = (acc_k[...] + acc_kt[...].T).astype(BF)

        @pl.when(me + 1 < blocks)
        def _():
            copy.wait_recv()

        @pl.when(me + 1 == blocks)
        def _():
            after[...] = jnp.zeros_like(after)

        rows = jnp.concatenate([tail[...], after[...]], axis=0).astype(F32)
        gv_ref[length - EDGE :] = back_conv(rows, taps_ref[...])[:EDGE]

        @pl.when(me > 0)
        def _():
            copy.wait_send()


def call(body, steps, in_specs, out_specs, out_shape, scratch=(), collective_id=None):
    remote = {} if collective_id is None else dict(
        collective_id=collective_id, has_side_effects=True
    )
    return pl.pallas_call(
        body,
        grid=(steps,),
        in_specs=in_specs,
        out_specs=out_specs,
        out_shape=out_shape,
        scratch_shapes=list(scratch),
        compiler_params=pltpu.CompilerParams(
            dimension_semantics=("arbitrary",), vmem_limit_bytes=LIMIT, **remote
        ),
    )


def per_device(width, queries, keys, values, conv_weight, gain, cotangent):
    length, channels = values.shape
    heads = queries.shape[1] // FEAT
    feats = heads * FEAT
    blocks = lax.axis_size("ctx")
    shape = jax.ShapeDtypeStruct
    peers = lax.axis_size("head")
    col = pl.BlockSpec((length, 128), lambda h: (0, h))
    wide = pl.BlockSpec((length, 256), lambda h: (0, h))
    tok = pl.BlockSpec((length, feats), lambda h: (0, 0))
    feat = pl.BlockSpec((feats, length), lambda h: (0, 0))
    mine = pl.BlockSpec((FEAT, length), lambda h: (h, 0))
    state = pl.BlockSpec((1, ROWS, 128), lambda h: (h, 0, 0))
    states = pl.BlockSpec((heads, ROWS, 128), lambda h: (0, 0, 0))
    priors = pl.BlockSpec((heads, ROWS, 256), lambda h: (0, 0, 0))
    sums = pl.BlockSpec((ROWS, 128), lambda h: (0, 0))
    vec = pl.BlockSpec((1, 128), lambda h: (0, h))
    pad = pl.BlockSpec((length, 128), lambda h: (0, 0))

    def early(i):
        return i % heads * (1 - i // heads) + i // heads * (heads - 1)

    def late(i):
        return i // heads * (i % heads)

    gain2 = gain.reshape(1, channels)

    conv, local, local_sum, qt, kt = call(
        functools.partial(state_kernel, blocks),
        heads,
        [
            pl.BlockSpec(memory_space=pl.ANY),
            col,
            pl.BlockSpec((CONV, 128), lambda h: (0, h)),
            tok,
            tok,
        ],
        [col, state, sums, feat, feat],
        [
            shape((length, channels), BF),
            shape((heads, ROWS, 128), BF),
            shape((ROWS, 128), F32),
            shape((feats, length), BF),
            shape((feats, length), BF),
        ],
        [
            pltpu.VMEM((EDGE, channels), BF),
            pltpu.SemaphoreType.DMA,
            pltpu.SemaphoreType.DMA,
        ],
        2,
    )(values, values, conv_weight, queries, keys)

    att, den, stat, prior = call(
        functools.partial(forward_kernel, blocks, peers, heads),
        2 * heads,
        [
            states,
            sums,
            tok,
            feat,
            pl.BlockSpec((FEAT, length), lambda i: (late(i), 0)),
            pl.BlockSpec((length, 128), lambda i: (0, early(i))),
            pl.BlockSpec((length, 128), lambda i: (0, late(i))),
            pl.BlockSpec((1, 128), lambda i: (0, late(i))),
        ],
        [pl.BlockSpec((length, 128), lambda i: (0, late(i))), pad, pad, priors],
        [
            shape((length, channels), F32),
            shape((length, 128), F32),
            shape((length, 128), F32),
            shape((heads, ROWS, 256), BF),
        ],
        [
            pltpu.VMEM((length, 128), F32),
            pltpu.VMEM((heads, length, 256), F32),
            pltpu.VMEM((8, length), F32),
            pltpu.VMEM((max(peers - 1, 1), 8, length), F32),
            pltpu.SemaphoreType.DMA((max(peers - 1, 1),)),
            pltpu.SemaphoreType.DMA((max(peers - 1, 1),)),
        ]
        + exchange_scratch(blocks, heads),
        0,
    )(local, local_sum, queries, kt, qt, conv, cotangent, gain2)

    normed, dn, back, back_sum = call(
        functools.partial(norm_kernel, width),
        heads,
        [col, pad, pad, col, vec, mine],
        [col, wide, state, sums],
        [
            shape((length, channels), BF),
            shape((length, heads * 256), BF),
            shape((heads, ROWS, 128), BF),
            shape((ROWS, 128), F32),
        ],
    )(att, den, stat, cotangent, gain2, qt)

    grad_q, grad_k, grad_v = call(
        functools.partial(backward_kernel, blocks, heads),
        2 * heads,
        [
            states,
            sums,
            tok,
            tok,
            feat,
            pl.BlockSpec((FEAT, length), lambda i: (early(i), 0)),
            pl.BlockSpec((FEAT, length), lambda i: (i % heads, 0)),
            pl.BlockSpec((length, 128), lambda i: (0, i % heads)),
            pl.BlockSpec((length, 256), lambda i: (0, early(i))),
            pl.BlockSpec((1, ROWS, 256), lambda i: (early(i), 0, 0)),
            pl.BlockSpec((CONV, channels), lambda i: (0, 0)),
        ],
        [tok, tok, pl.BlockSpec((length, channels), lambda i: (0, 0))],
        [
            shape((length, feats), BF),
            shape((length, feats), BF),
            shape((length, channels), BF),
        ],
        [
            pltpu.VMEM((feats, length), F32),
            pltpu.VMEM((feats, length), F32),
            pltpu.VMEM((length, feats), F32),
            pltpu.VMEM((heads, length, 128), F32),
            pltpu.VMEM((heads, ROWS, 256), BF),
        ]
        + [pltpu.VMEM((EDGE, channels), BF)] * 3
        + [pltpu.SemaphoreType.DMA] * 2
        + exchange_scratch(blocks, heads),
        1,
    )(back, back_sum, queries, keys, qt, qt, kt, conv, dn, prior, conv_weight)
    return (normed, grad_q, grad_k, grad_v)


def solution(mesh):
    two = P("ctx", "head")

    def run(queries, keys, values, conv_weight, gain, cotangent):
        return jax.shard_map(
            functools.partial(per_device, values.shape[1]),
            mesh=mesh,
            in_specs=(two, two, two, P(None, "head"), P("head"), two),
            out_specs=(two, two, two, two),
            check_vma=False,
        )(queries, keys, values, conv_weight, gain, cotangent)

    return run
```
